256 devices in a mesh: ctx: 32 (over z, y_hi, core), chan: 8 (over x, y_lo).
Axes of the slice: x: 4, y: 4 (y_hi: 2, y_lo: 2; y = y_hi * 2 + y_lo), z: 8, core: 2. Of those that a mesh axis runs over, the one named last changes fastest.
Arguments:
- query_gate: bfloat16 [16384, 4096], P('ctx', 'chan'), may hold values from -600 to 600
- key_branch: bfloat16 [16384, 4096], P('ctx', 'chan'), may hold values from -6 to 6
- value_branch: bfloat16 [16384, 4096], P('ctx', 'chan'), may hold values from -6 to 6
- conv_filter: float32 [16384, 4096], P('ctx', 'chan'), may hold values from -1.1 to 1.1
- skip_weight: float32 [4096], P('chan'), may hold values from 0.5 to 1.5
- norm_gain: float32 [4096], P('chan'), may hold values from 0.25 to 1.75
Outputs:
- layer_out: bfloat16 [16384, 4096], P('ctx', 'chan')
The draws below stay inside these ranges and needn't reach their ends.
All inputs are finite; a program needn't handle non-finite values.
Results may differ from the reference program's by a relative error of at most 0.0022.
Values sent between devices are 32-bit elements; how exact they have to be, the bound alone decides.
No kernel may reach another device: no remote copies, remote signals or barrier semaphores. Data moves between devices by JAX's collectives and lax.ppermute only.
A program may use at most 128 MiB of HBM per device.

```python
import math
import jax
import jax.numpy as jnp
from jax import lax

CH = 4096
SEQ = 16384


def draw_query_gate(key, part):
    key = jax.random.fold_in(key, 11)
    key_noise = jax.random.fold_in(key, 0)
    key_row = jax.random.fold_in(key, 2)
    channel_pos = jnp.arange(CH, dtype=jnp.float32) / (CH - 1)
    jitter = jax.random.truncated_normal(key_noise, -4.0, 4.0, (SEQ, CH), jnp.float32)
    column = jnp.exp(jnp.log(10.0) * channel_pos)
    row_scale = jnp.exp(jax.random.uniform(key_row, (SEQ, 1), jnp.float32, 0.0, jnp.log(10.0)))
    return (jitter * column[None, :] * row_scale).astype(jnp.bfloat16)


def draw_conv_filter(key, part):
    key = jax.random.fold_in(key, 23)
    key_noise, key_pick, key_slow, key_fast = jax.random.split(key, 4)
    slow_share = 0.5
    is_slow = jax.random.uniform(key_pick, (CH,), jnp.float32) < slow_share
    slow_rates = jnp.exp(jax.random.uniform(key_slow, (CH,), jnp.float32, jnp.log(0.2 / SEQ), jnp.log(2.0 / SEQ)))
    fast_rates = jnp.exp(jax.random.uniform(key_fast, (CH,), jnp.float32, jnp.log(1.0 / 50.0), jnp.log(1.0 / 30.0)))
    rates = jnp.where(is_slow, slow_rates, fast_rates)
    amplitude = jnp.sqrt(jnp.expm1(-2.0 * rates) / jnp.expm1(-2.0 * rates * SEQ))
    positions = jnp.arange(SEQ, dtype=jnp.float32)
    jitter = jax.random.truncated_normal(key_noise, -4.0, 4.0, (SEQ, CH), jnp.float32)
    return jitter * amplitude[None, :] * jnp.exp(-rates[None, :] * positions[:, None])


def steps_of(own_key, dims, cuts, low, largest):
    gain = 1.0
    for position, shards_of in cuts:
        heights = jax.random.uniform(jax.random.fold_in(jax.random.fold_in(own_key, 6), position), (shards_of,), jnp.float32, low / len(cuts), largest / len(cuts))
        gain = gain * jnp.repeat(jnp.exp(heights), dims[position] // shards_of).reshape((-1,) + (1,) * (len(dims) - 1 - position))
    return gain


def noise(key, extent, scale, most, shards=(), held_as=jnp.bfloat16):
    array = jax.random.normal(key, extent, jnp.float32) * scale
    if len(shards) > 0:
        array = steps_of(key, extent, shards, -0.22, 0.18) * array
    return jnp.clip(array, min=-most, max=most).astype(held_as)


def setup_inputs(seed: int = 0) -> dict:
    seeds = jax.random.split(jax.random.key(seed), 7)
    return {
        "query_gate": draw_query_gate(jax.random.fold_in(seeds[6], 71), 0),
        "key_branch": noise(seeds[1], (SEQ, CH), 1.0, 6.0, ((0, 32), (1, 8))),
        "value_branch": noise(seeds[2], (SEQ, CH), 1.0, 6.0, ((0, 32), (1, 8))),
        "conv_filter": draw_conv_filter(jax.random.fold_in(seeds[6], 71), 0),
        "skip_weight": jnp.clip(0.5 + 1.0 * jax.random.uniform(seeds[4], (CH,), jnp.float32) ** steps_of(seeds[4], (CH,), ((0, 8),), -0.2, 0.2), 0.5, 1.5),
        "norm_gain": jnp.clip(1.0 + 0.15 * jax.random.normal(seeds[5], (CH,), jnp.float32), 0.25, 1.75),
    }


def convolve_group(arrays):
    signal, kernel = arrays
    length = 2 * SEQ
    spectrum = jnp.fft.rfft(signal, n=length, axis=0) * jnp.fft.rfft(kernel, n=length, axis=0)
    return jnp.fft.irfft(spectrum, n=length, axis=0)[:SEQ]

def reference(query_gate, key_branch, value_branch, conv_filter, skip_weight, norm_gain):
    product = key_branch.astype(jnp.float32) * value_branch.astype(jnp.float32)
    per_map = math.gcd(CH, 256)
    groups = CH // per_map
    signal = product.reshape(SEQ, groups, per_map).transpose(1, 0, 2)
    kernel = conv_filter.astype(jnp.float32).reshape(SEQ, groups, per_map).transpose(1, 0, 2)
    convolved = lax.map(convolve_group, (signal, kernel))
    convolved = convolved.transpose(1, 0, 2).reshape(SEQ, CH).astype(jnp.float32)
    gated = query_gate.astype(jnp.float32) * (convolved + skip_weight[None, :] * product)
    mean_square = lax.optimization_barrier(jnp.mean(gated * gated, axis=1, keepdims=True))
    return (gated * lax.rsqrt(mean_square + 1e-05) * norm_gain[None, :]).astype(jnp.bfloat16)
```

```python
import functools
import math

import jax
import jax.numpy as jnp
import ml_dtypes
import numpy as np
from jax import lax
from jax.experimental import pallas as pl
from jax.experimental.pallas import tpu as pltpu
from jax.sharding import PartitionSpec as P

CH = 4096
LANES = 128
F32 = jnp.float32
BF16 = jnp.bfloat16
VMEM_BYTES = 32 * 1024 * 1024


def split_const(values):
    high = values.astype(ml_dtypes.bfloat16)
    low = (values - high.astype(np.float64)).astype(ml_dtypes.bfloat16)
    return high, low


def transform_tables(rows, cols):
    length = rows * cols
    m = np.arange(rows, dtype=np.float64)
    b = np.arange(cols, dtype=np.float64)
    first = 2.0 * math.pi * np.outer(m + 0.25, m) / rows
    first_high, first_low = split_const(np.concatenate([np.cos(first), -np.sin(first)], axis=0))
    first_table = np.concatenate([first_high, first_high, first_low], axis=1)
    turn = 2.0 * math.pi * np.outer(m + 0.25, b) / length
    turn_re = np.cos(turn).astype(np.float32)
    turn_im = (-np.sin(turn)).astype(np.float32)
    second = 2.0 * math.pi * (np.outer(b, b) % cols) / cols
    cosine, sine = np.cos(second), np.sin(second)
    fwd_high, fwd_low = split_const(np.block([[cosine, -sine], [sine, cosine]]))
    fwd_table = np.concatenate([fwd_high, fwd_high, fwd_low], axis=0)
    back_high, back_low = split_const(np.block([[cosine, sine], [-sine, cosine]]))
    back_table = np.concatenate([back_high, back_high, back_low], axis=0)
    last_high, last_low = split_const(
        np.concatenate([np.cos(first.T), -np.sin(first.T)], axis=1) / length
    )
    last_table = np.concatenate([last_high, last_high, last_low], axis=1)
    return first_table, turn_re, turn_im, fwd_table, back_table, last_table


def split(values):
    high = values.astype(BF16)
    low = (values - high.astype(F32)).astype(BF16)
    return high, low


def dot(left, right):
    return jnp.dot(left, right, preferred_element_type=F32)


def pack_kernel(key_ref, value_ref, filter_ref, out_ref):
    share = out_ref.shape[3]
    product = key_ref[...].astype(F32) * value_ref[...].astype(F32)
    out_ref[:, 0, 0] = product.T.reshape(-1, share, LANES)
    out_ref[:, 0, 1] = filter_ref[...].T.reshape(-1, share, LANES)


def conv_kernel(
    group, share, data_ref, first_ref, turn_re_ref, turn_im_ref, fwd_ref, back_ref, last_ref, out_ref
):
    rows = turn_re_ref.shape[0]
    turn_re = jnp.concatenate([turn_re_ref[...]] * 2, axis=1)
    turn_im = jnp.concatenate([turn_im_ref[...]] * 2, axis=1)
    for start in range(0, share, group):
        parts = []
        for c in range(start, start + group):
            signal = data_ref[pl.ds(c, rows, stride=2 * share), :]
            kernel = data_ref[pl.ds(share + c, rows, stride=2 * share), :]
            high, low = split(jnp.concatenate([signal, kernel], axis=1))
            spec = dot(first_ref[...], jnp.concatenate([high, low, high], axis=0))
            re, im = spec[:rows], spec[rows:]
            out_re = re * turn_re - im * turn_im
            out_im = re * turn_im + im * turn_re
            parts.append(jnp.concatenate([out_re[:, :LANES], out_im[:, :LANES]], axis=1))
            parts.append(jnp.concatenate([out_re[:, LANES:], out_im[:, LANES:]], axis=1))
        high, low = split(jnp.concatenate(parts, axis=0))
        spec = dot(jnp.concatenate([high, low, high], axis=1), fwd_ref[...])
        parts = []
        for c in range(group):
            signal = spec[2 * c * rows : (2 * c + 1) * rows]
            kernel = spec[(2 * c + 1) * rows : (2 * c + 2) * rows]
            s_re, s_im = signal[:, :LANES], signal[:, LANES:]
            k_re, k_im = kernel[:, :LANES], kernel[:, LANES:]
            parts.append(
                jnp.concatenate([s_re * k_re - s_im * k_im, s_re * k_im + s_im * k_re], axis=1)
            )
        high, low = split(jnp.concatenate(parts, axis=0))
        spec = dot(jnp.concatenate([high, low, high], axis=1), back_ref[...])
        for c in range(0, group, 2):
            first = spec[c * rows : (c + 1) * rows]
            second = spec[(c + 1) * rows : (c + 2) * rows]
            re = jnp.concatenate([first[:, :LANES], second[:, :LANES]], axis=1)
            im = jnp.concatenate([first[:, LANES:], second[:, LANES:]], axis=1)
            turned = jnp.concatenate(
                [re * turn_re + im * turn_im, im * turn_re - re * turn_im], axis=0
            )
            high, low = split(turned)
            conv = dot(last_ref[...], jnp.concatenate([high, low, high], axis=0))
            out_ref[pl.ds(start + c, rows, stride=share), :] = conv[:, :LANES]
            out_ref[pl.ds(start + c + 1, rows, stride=share), :] = conv[:, LANES:]


def gate_kernel(conv_ref, query_ref, key_ref, value_ref, skip_ref, gated_ref, square_ref):
    conv = conv_ref[...].reshape(-1, LANES).T
    product = key_ref[...].astype(F32) * value_ref[...].astype(F32)
    gated = query_ref[...].astype(F32) * (conv + skip_ref[...] * product)
    gated_ref[...] = gated
    square = gated * gated
    folded = square[:, :LANES]
    for start in range(LANES, square.shape[1], LANES):
        folded = folded + square[:, start : start + LANES]
    total = jnp.sum(folded.T, axis=0, keepdims=True)
    square_ref[...] = jnp.broadcast_to(total, square_ref.shape)


def norm_kernel(gated_ref, square_ref, gain_ref, out_ref):
    total = jnp.sum(square_ref[...], axis=0, keepdims=True)
    inverse = lax.rsqrt(total / CH + 1e-05)
    spread = jnp.broadcast_to(inverse, (LANES, LANES)).T
    for start in range(0, out_ref.shape[1], LANES):
        at = slice(start, start + LANES)
        out_ref[:, at] = (gated_ref[:, at] * spread * gain_ref[:, at]).astype(BF16)


def on_device(query_gate, key_branch, value_branch, conv_filter, skip_weight, norm_gain):
    blocks = lax.axis_size("ctx")
    peers = lax.axis_size("chan")
    tokens, channels = key_branch.shape
    share = channels // blocks
    pieces = tokens // LANES
    rows = blocks * pieces
    params = pltpu.CompilerParams(vmem_limit_bytes=VMEM_BYTES)
    strip = pl.BlockSpec((LANES, channels), lambda a: (a, 0))
    row = pl.BlockSpec((1, channels), lambda a: (0, 0))
    packed = pl.pallas_call(
        pack_kernel,
        grid=(pieces,),
        in_specs=[strip] * 3,
        out_specs=pl.BlockSpec((blocks, 1, 2, share, LANES), lambda a: (0, a, 0, 0, 0)),
        out_shape=jax.ShapeDtypeStruct((blocks, pieces, 2, share, LANES), F32),
        compiler_params=params,
        name="pack",
    )(key_branch, value_branch, conv_filter)
    packed = packed.reshape(blocks, pieces * 2 * share, LANES)
    gathered = lax.all_to_all(packed, "ctx", split_axis=0, concat_axis=0, tiled=True)
    gathered = gathered.reshape(rows * 2 * share, LANES)
    tables = transform_tables(rows, LANES)
    conv = pl.pallas_call(
        functools.partial(conv_kernel, 4, share),
        out_shape=jax.ShapeDtypeStruct((rows * share, LANES), F32),
        compiler_params=params,
        name="conv",
    )(gathered, *tables)
    conv = conv.reshape(blocks, pieces * share, LANES)
    conv = lax.all_to_all(conv, "ctx", split_axis=0, concat_axis=0, tiled=True)
    conv = conv.reshape(blocks, pieces, share, LANES)
    gated, square = pl.pallas_call(
        gate_kernel,
        grid=(pieces,),
        in_specs=[
            pl.BlockSpec((blocks, 1, share, LANES), lambda a: (0, a, 0, 0)),
            strip,
            strip,
            strip,
            row,
        ],
        out_specs=[strip, pl.BlockSpec((peers, LANES), lambda a: (0, a))],
        out_shape=[
            jax.ShapeDtypeStruct((tokens, channels), F32),
            jax.ShapeDtypeStruct((peers, tokens), F32),
        ],
        compiler_params=params,
        name="gate",
    )(conv, query_gate, key_branch, value_branch, skip_weight[None])
    square = lax.all_to_all(square, "chan", split_axis=0, concat_axis=0, tiled=True)
    return pl.pallas_call(
        norm_kernel,
        grid=(pieces,),
        in_specs=[strip, pl.BlockSpec((peers, LANES), lambda a: (0, a)), row],
        out_specs=strip,
        out_shape=jax.ShapeDtypeStruct((tokens, channels), BF16),
        compiler_params=params,
        name="norm",
    )(gated, square, norm_gain[None])


def solution(mesh):
    wide = P("ctx", "chan")
    return jax.shard_map(
        on_device,
        mesh=mesh,
        in_specs=(wide, wide, wide, wide, P("chan"), P("chan")),
        out_specs=wide,
        check_vma=False,
    )
```

```python
import functools
import math

import jax
import jax.numpy as jnp
import ml_dtypes
import numpy as np
from jax import lax
from jax.experimental import pallas as pl
from jax.experimental.pallas import tpu as pltpu
from jax.sharding import PartitionSpec as P

CH = 4096
LANES = 128
F32 = jnp.float32
BF16 = jnp.bfloat16
VMEM_BYTES = 32 * 1024 * 1024
PACK_VMEM_BYTES = 56 * 1024 * 1024


def split_const(values):
    high = values.astype(ml_dtypes.bfloat16)
    low = (values - high.astype(np.float64)).astype(ml_dtypes.bfloat16)
    return high, low


def transform_tables(rows, cols):
    length = rows * cols
    m = np.arange(rows, dtype=np.float64)
    b = np.arange(cols, dtype=np.float64)
    first = 2.0 * math.pi * np.outer(m + 0.25, m) / rows
    first_high, first_low = split_const(np.concatenate([np.cos(first), -np.sin(first)], axis=0))
    first_table = np.concatenate([first_high, first_high, first_low], axis=1)
    turn = 2.0 * math.pi * np.outer(m + 0.25, b) / length
    turn_re = np.cos(turn).astype(np.float32)
    turn_im = (-np.sin(turn)).astype(np.float32)
    second = 2.0 * math.pi * (np.outer(b, b) % cols) / cols
    cosine, sine = np.cos(second), np.sin(second)
    fwd_high, fwd_low = split_const(np.block([[cosine, -sine], [sine, cosine]]))
    fwd_table = np.concatenate([fwd_high, fwd_high, fwd_low], axis=0)
    back_high, back_low = split_const(np.block([[cosine, sine], [-sine, cosine]]))
    back_table = np.concatenate([back_high, back_high, back_low], axis=0)
    last_high, last_low = split_const(
        np.concatenate([np.cos(first.T), -np.sin(first.T)], axis=1) / length
    )
    last_table = np.concatenate([last_high, last_high, last_low], axis=1)
    return first_table, turn_re, turn_im, fwd_table, back_table, last_table


def split(values):
    high = values.astype(BF16)
    low = (values - high.astype(F32)).astype(BF16)
    return high, low


def dot(left, right):
    return jnp.dot(left, right, preferred_element_type=F32)


def pack_kernel(
    key_hbm, value_hbm, filter_hbm, out_hbm, key_ref, value_ref, filter_ref, out_ref, sems, out_sems
):
    pieces, share = out_ref.shape[1], out_ref.shape[3]
    pairs = ((key_hbm, key_ref), (value_hbm, value_ref), (filter_hbm, filter_ref))
    copies = []
    for piece in range(pieces):
        at = pl.ds(piece * LANES, LANES)
        for index, (source, target) in enumerate(pairs):
            copies.append(
                pltpu.make_async_copy(source.at[at], target.at[at], sems.at[piece, index])
            )
    for copy in copies:
        copy.start()
    sends = []
    for piece in range(pieces):
        at = pl.ds(piece * LANES, LANES)
        copies[3 * piece].wait()
        copies[3 * piece + 1].wait()
        product = key_ref[at, :].astype(F32) * value_ref[at, :].astype(F32)
        out_ref[:, piece, 0] = product.T.reshape(-1, share, LANES)
        copies[3 * piece + 2].wait()
        out_ref[:, piece, 1] = filter_ref[at, :].T.reshape(-1, share, LANES)
        sends.append(
            pltpu.make_async_copy(out_ref.at[:, piece], out_hbm.at[:, piece], out_sems.at[piece])
        )
        sends[-1].start()
    for send in sends:
        send.wait()


def conv_kernel(
    group, share, data_ref, first_ref, turn_re_ref, turn_im_ref, fwd_ref, back_ref, last_ref, out_ref
):
    rows = turn_re_ref.shape[0]
    turn_re = jnp.concatenate([turn_re_ref[...]] * 2, axis=1)
    turn_im = jnp.concatenate([turn_im_ref[...]] * 2, axis=1)

    def over_rows(table_ref, values):
        high, low = split(values)
        return dot(table_ref[...], jnp.concatenate([high, low, high], axis=0))

    def over_lanes(values, table_ref):
        high, low = split(values)
        return dot(jnp.concatenate([high, low, high], axis=1), table_ref[...])

    def first_stage(start):
        parts = []
        for c in range(start, start + group):
            signal = data_ref[pl.ds(c, rows, stride=2 * share), :]
            kernel = data_ref[pl.ds(share + c, rows, stride=2 * share), :]
            spec = over_rows(first_ref, jnp.concatenate([signal, kernel], axis=1))
            re, im = spec[:rows], spec[rows:]
            out_re = re * turn_re - im * turn_im
            out_im = re * turn_im + im * turn_re
            parts.append(jnp.concatenate([out_re[:, :LANES], out_im[:, :LANES]], axis=1))
            parts.append(jnp.concatenate([out_re[:, LANES:], out_im[:, LANES:]], axis=1))
        return jnp.concatenate(parts, axis=0)

    def product_of_spectra(turned):
        spec = over_lanes(turned, fwd_ref)
        parts = []
        for c in range(group):
            signal = spec[2 * c * rows : (2 * c + 1) * rows]
            kernel = spec[(2 * c + 1) * rows : (2 * c + 2) * rows]
            s_re, s_im = signal[:, :LANES], signal[:, LANES:]
            k_re, k_im = kernel[:, :LANES], kernel[:, LANES:]
            parts.append(
                jnp.concatenate([s_re * k_re - s_im * k_im, s_re * k_im + s_im * k_re], axis=1)
            )
        return jnp.concatenate(parts, axis=0)

    def last_stage(spec, start):
        for c in range(0, group, 2):
            first = spec[c * rows : (c + 1) * rows]
            second = spec[(c + 1) * rows : (c + 2) * rows]
            re = jnp.concatenate([first[:, :LANES], second[:, :LANES]], axis=1)
            im = jnp.concatenate([first[:, LANES:], second[:, LANES:]], axis=1)
            turned = jnp.concatenate(
                [re * turn_re + im * turn_im, im * turn_re - re * turn_im], axis=0
            )
            conv = over_rows(last_ref, turned)
            out_ref[pl.ds(start + c, rows, stride=share), :] = conv[:, :LANES]
            out_ref[pl.ds(start + c + 1, rows, stride=share), :] = conv[:, LANES:]

    groups = share // group
    turned, spectra, back = {}, {}, {}
    for step in range(groups + 3):
        if step < groups:
            turned[step] = first_stage(step * group)
        if 0 <= step - 1 < groups:
            spectra[step - 1] = product_of_spectra(turned.pop(step - 1))
        if 0 <= step - 2 < groups:
            back[step - 2] = over_lanes(spectra.pop(step - 2), back_ref)
        if 0 <= step - 3 < groups:
            last_stage(back.pop(step - 3), (step - 3) * group)


def gate_kernel(conv_ref, query_ref, key_ref, value_ref, skip_ref, gated_ref, square_ref):
    conv = conv_ref[...].reshape(-1, LANES).T
    product = key_ref[...].astype(F32) * value_ref[...].astype(F32)
    gated = query_ref[...].astype(F32) * (conv + skip_ref[...] * product)
    gated_ref[...] = gated
    square = gated * gated
    folded = square[:, :LANES]
    for start in range(LANES, square.shape[1], LANES):
        folded = folded + square[:, start : start + LANES]
    total = jnp.sum(folded.T, axis=0, keepdims=True)
    square_ref[...] = jnp.broadcast_to(total, square_ref.shape)


def norm_kernel(gated_ref, square_ref, gain_ref, out_ref):
    total = jnp.sum(square_ref[...], axis=0, keepdims=True)
    inverse = lax.rsqrt(total / CH + 1e-05)
    for top in range(0, out_ref.shape[0], LANES):
        down = slice(top, top + LANES)
        spread = jnp.broadcast_to(inverse[:, down], (LANES, LANES)).T
        for start in range(0, out_ref.shape[1], LANES):
            at = slice(start, start + LANES)
            out_ref[down, at] = (gated_ref[down, at] * spread * gain_ref[:, at]).astype(BF16)


def on_device(query_gate, key_branch, value_branch, conv_filter, skip_weight, norm_gain):
    blocks = lax.axis_size("ctx")
    peers = lax.axis_size("chan")
    tokens, channels = key_branch.shape
    share = channels // blocks
    pieces = tokens // LANES
    rows = blocks * pieces
    params = pltpu.CompilerParams(vmem_limit_bytes=VMEM_BYTES)
    strip = pl.BlockSpec((LANES, channels), lambda a: (a, 0))
    row = pl.BlockSpec((1, channels), lambda a: (0, 0))
    whole = (tokens, channels)
    whole = (tokens, channels)
    packed_shape = (blocks, pieces, 2, share, LANES)
    packed = pl.pallas_call(
        pack_kernel,
        in_specs=[pl.BlockSpec(memory_space=pltpu.HBM)] * 3,
        out_specs=pl.BlockSpec(memory_space=pltpu.HBM),
        out_shape=jax.ShapeDtypeStruct(packed_shape, F32),
        scratch_shapes=[
            pltpu.VMEM(whole, BF16),
            pltpu.VMEM(whole, BF16),
            pltpu.VMEM(whole, F32),
            pltpu.VMEM(packed_shape, F32),
            pltpu.SemaphoreType.DMA((pieces, 3)),
            pltpu.SemaphoreType.DMA((pieces,)),
        ],
        compiler_params=pltpu.CompilerParams(vmem_limit_bytes=PACK_VMEM_BYTES),
        name="pack",
    )(key_branch, value_branch, conv_filter)
    packed = packed.reshape(blocks, pieces * 2 * share, LANES)
    gathered = lax.all_to_all(packed, "ctx", split_axis=0, concat_axis=0, tiled=True)
    gathered = gathered.reshape(rows * 2 * share, LANES)
    tables = transform_tables(rows, LANES)
    conv = pl.pallas_call(
        functools.partial(conv_kernel, 4, share),
        out_shape=jax.ShapeDtypeStruct((rows * share, LANES), F32),
        compiler_params=params,
        name="conv",
    )(gathered, *tables)
    conv = conv.reshape(blocks, pieces * share, LANES)
    conv = lax.all_to_all(conv, "ctx", split_axis=0, concat_axis=0, tiled=True)
    conv = conv.reshape(blocks, pieces, share, LANES)
    gated, square = pl.pallas_call(
        gate_kernel,
        grid=(pieces,),
        in_specs=[
            pl.BlockSpec((blocks, 1, share, LANES), lambda a: (0, a, 0, 0)),
            strip,
            strip,
            strip,
            row,
        ],
        out_specs=[strip, pl.BlockSpec((peers, LANES), lambda a: (0, a))],
        out_shape=[
            jax.ShapeDtypeStruct((tokens, channels), F32),
            jax.ShapeDtypeStruct((peers, tokens), F32),
        ],
        compiler_params=params,
        name="gate",
    )(conv, query_gate, key_branch, value_branch, skip_weight[None])
    square = lax.all_to_all(square, "chan", split_axis=0, concat_axis=0, tiled=True)
    return pl.pallas_call(
        norm_kernel,
        out_shape=jax.ShapeDtypeStruct((tokens, channels), BF16),
        compiler_params=params,
        name="norm",
    )(gated, square, norm_gain[None])


def solution(mesh):
    wide = P("ctx", "chan")
    return jax.shard_map(
        on_device,
        mesh=mesh,
        in_specs=(wide, wide, wide, wide, P("chan"), P("chan")),
        out_specs=wide,
        check_vma=False,
    )
```

```python
import functools
import math

import jax
import jax.numpy as jnp
import ml_dtypes
import numpy as np
from jax import lax
from jax.experimental import pallas as pl
from jax.experimental.pallas import tpu as pltpu
from jax.sharding import PartitionSpec as P

CH = 4096
LANES = 128
F32 = jnp.float32
BF16 = jnp.bfloat16
VMEM_BYTES = 32 * 1024 * 1024
PACK_VMEM_BYTES = 56 * 1024 * 1024


def split_const(values):
    high = values.astype(ml_dtypes.bfloat16)
    low = (values - high.astype(np.float64)).astype(ml_dtypes.bfloat16)
    return high, low


def transform_tables(rows, cols):
    length = rows * cols
    m = np.arange(rows, dtype=np.float64)
    b = np.arange(cols, dtype=np.float64)
    first = 2.0 * math.pi * np.outer(m + 0.25, m) / rows
    first_high, first_low = split_const(np.concatenate([np.cos(first), -np.sin(first)], axis=0))
    first_table = np.block([[first_high, first_high], [first_low, np.zeros_like(first_low)]])
    turn = 2.0 * math.pi * np.outer(m + 0.25, b) / length
    turn_re = np.cos(turn).astype(np.float32)
    turn_im = (-np.sin(turn)).astype(np.float32)
    second = 2.0 * math.pi * (np.outer(b, b) % cols) / cols
    cosine, sine = np.cos(second), np.sin(second)
    fwd_high, fwd_low = split_const(np.block([[cosine, -sine], [sine, cosine]]))
    fwd_table = np.concatenate([fwd_high, fwd_high, fwd_low], axis=0)
    back_high, back_low = split_const(np.block([[cosine, sine], [-sine, cosine]]))
    back_table = np.concatenate([back_high, back_high, back_low], axis=0)
    last_high, last_low = split_const(
        np.concatenate([np.cos(first.T), -np.sin(first.T)], axis=1) / length
    )
    last_table = np.concatenate([last_high, last_low], axis=0)
    return first_table, turn_re, turn_im, fwd_table, back_table, last_table


def split(values):
    high = values.astype(BF16)
    low = (values - high.astype(F32)).astype(BF16)
    return high, low


def dot(left, right):
    return jnp.dot(left, right, preferred_element_type=F32)


def pack_kernel(
    key_hbm, value_hbm, filter_hbm, out_hbm, key_ref, value_ref, filter_ref, out_ref, sems, out_sems
):
    pieces, share = out_ref.shape[1], out_ref.shape[3]
    pairs = ((key_hbm, key_ref), (value_hbm, value_ref), (filter_hbm, filter_ref))
    copies = []
    for piece in range(pieces):
        at = pl.ds(piece * LANES, LANES)
        for index, (source, target) in enumerate(pairs):
            copies.append(
                pltpu.make_async_copy(source.at[at], target.at[at], sems.at[piece, index])
            )
    for copy in copies:
        copy.start()
    sends = []

    def send(piece, stream):
        sends.append(
            pltpu.make_async_copy(
                out_ref.at[:, piece, stream],
                out_hbm.at[:, piece, stream],
                out_sems.at[piece, stream],
            )
        )
        sends[-1].start()

    for piece in range(pieces):
        at = pl.ds(piece * LANES, LANES)
        copies[3 * piece].wait()
        copies[3 * piece + 1].wait()
        product = key_ref[at, :].astype(F32) * value_ref[at, :].astype(F32)
        out_ref[:, piece, 0] = product.T.reshape(-1, share, LANES)
        send(piece, 0)
        copies[3 * piece + 2].wait()
        out_ref[:, piece, 1] = filter_ref[at, :].T.reshape(-1, share, LANES)
        send(piece, 1)
    for copy in sends:
        copy.wait()


def conv_kernel(
    group, share, data_ref, first_ref, turn_re_ref, turn_im_ref, fwd_ref, back_ref, last_ref, out_ref
):
    rows = turn_re_ref.shape[0]
    turn_re = jnp.concatenate([turn_re_ref[...]] * 2, axis=1)
    turn_im = jnp.concatenate([turn_im_ref[...]] * 2, axis=1)

    def over_lanes(values, table_ref):
        high, low = split(values)
        return dot(jnp.concatenate([high, low, high], axis=1), table_ref[...])

    def first_stage(start):
        parts = []
        for c in range(start, start + group):
            signal = data_ref[pl.ds(c, rows, stride=2 * share), :]
            kernel = data_ref[pl.ds(share + c, rows, stride=2 * share), :]
            high, low = split(jnp.concatenate([signal, kernel], axis=1))
            spec = dot(first_ref[...], jnp.concatenate([high, low], axis=0))
            re = spec[:rows] + spec[2 * rows : 3 * rows]
            im = spec[rows : 2 * rows] + spec[3 * rows :]
            out_re = re * turn_re - im * turn_im
            out_im = re * turn_im + im * turn_re
            parts.append(jnp.concatenate([out_re[:, :LANES], out_im[:, :LANES]], axis=1))
            parts.append(jnp.concatenate([out_re[:, LANES:], out_im[:, LANES:]], axis=1))
        return jnp.concatenate(parts, axis=0)

    def product_of_spectra(turned):
        spec = over_lanes(turned, fwd_ref)
        parts = []
        for c in range(group):
            signal = spec[2 * c * rows : (2 * c + 1) * rows]
            kernel = spec[(2 * c + 1) * rows : (2 * c + 2) * rows]
            s_re, s_im = signal[:, :LANES], signal[:, LANES:]
            k_re, k_im = kernel[:, :LANES], kernel[:, LANES:]
            parts.append(
                jnp.concatenate([s_re * k_re - s_im * k_im, s_re * k_im + s_im * k_re], axis=1)
            )
        return jnp.concatenate(parts, axis=0)

    def last_stage(spec, start):
        for c in range(0, group, 2):
            first = spec[c * rows : (c + 1) * rows]
            second = spec[(c + 1) * rows : (c + 2) * rows]
            re = jnp.concatenate([first[:, :LANES], second[:, :LANES]], axis=1)
            im = jnp.concatenate([first[:, LANES:], second[:, LANES:]], axis=1)
            turned = jnp.concatenate(
                [re * turn_re + im * turn_im, im * turn_re - re * turn_im], axis=0
            )
            high, low = split(turned)
            conv = dot(last_ref[...], high)
            conv = conv[:rows] + dot(last_ref[:rows], low) + conv[rows:]
            out_ref[pl.ds(start + c, rows, stride=share), :] = conv[:, :LANES]
            out_ref[pl.ds(start + c + 1, rows, stride=share), :] = conv[:, LANES:]

    groups = share // group
    turned, spectra, back = {}, {}, {}
    for step in range(groups + 3):
        if 0 <= step - 1 < groups:
            spectra[step - 1] = product_of_spectra(turned.pop(step - 1))
        if step < groups:
            turned[step] = first_stage(step * group)
        if 0 <= step - 3 < groups:
            last_stage(back.pop(step - 3), (step - 3) * group)
        if 0 <= step - 2 < groups:
            back[step - 2] = over_lanes(spectra.pop(step - 2), back_ref)


def gate_kernel(conv_ref, query_ref, key_ref, value_ref, skip_ref, gated_ref, square_ref):
    for piece in range(conv_ref.shape[1]):
        at = slice(piece * LANES, (piece + 1) * LANES)
        conv = conv_ref[:, piece].reshape(-1, LANES).T
        product = key_ref[at, :].astype(F32) * value_ref[at, :].astype(F32)
        gated = query_ref[at, :].astype(F32) * (conv + skip_ref[...] * product)
        gated_ref[at, :] = gated
        square = gated * gated
        folded = square[:, :LANES]
        for start in range(LANES, square.shape[1], LANES):
            folded = folded + square[:, start : start + LANES]
        total = jnp.sum(folded.T, axis=0, keepdims=True)
        square_ref[:, at] = jnp.broadcast_to(total, (square_ref.shape[0], LANES))


def norm_kernel(gated_ref, square_ref, gain_ref, out_ref):
    total = jnp.sum(square_ref[...], axis=0, keepdims=True)
    inverse = lax.rsqrt(total / CH + 1e-05)
    for top in range(0, out_ref.shape[0], LANES):
        down = slice(top, top + LANES)
        spread = jnp.broadcast_to(inverse[:, down], (LANES, LANES)).T
        for start in range(0, out_ref.shape[1], LANES):
            at = slice(start, start + LANES)
            out_ref[down, at] = (gated_ref[down, at] * spread * gain_ref[:, at]).astype(BF16)


def on_device(query_gate, key_branch, value_branch, conv_filter, skip_weight, norm_gain):
    blocks = lax.axis_size("ctx")
    peers = lax.axis_size("chan")
    tokens, channels = key_branch.shape
    share = channels // blocks
    pieces = tokens // LANES
    rows = blocks * pieces
    params = pltpu.CompilerParams(vmem_limit_bytes=VMEM_BYTES)
    strip = pl.BlockSpec((LANES, channels), lambda a: (a, 0))
    row = pl.BlockSpec((1, channels), lambda a: (0, 0))
    whole = (tokens, channels)
    whole = (tokens, channels)
    packed_shape = (blocks, pieces, 2, share, LANES)
    packed = pl.pallas_call(
        pack_kernel,
        in_specs=[pl.BlockSpec(memory_space=pltpu.HBM)] * 3,
        out_specs=pl.BlockSpec(memory_space=pltpu.HBM),
        out_shape=jax.ShapeDtypeStruct(packed_shape, F32),
        scratch_shapes=[
            pltpu.VMEM(whole, BF16),
            pltpu.VMEM(whole, BF16),
            pltpu.VMEM(whole, F32),
            pltpu.VMEM(packed_shape, F32),
            pltpu.SemaphoreType.DMA((pieces, 3)),
            pltpu.SemaphoreType.DMA((pieces, 2)),
        ],
        compiler_params=pltpu.CompilerParams(vmem_limit_bytes=PACK_VMEM_BYTES),
        name="pack",
    )(key_branch, value_branch, conv_filter)
    packed = packed.reshape(blocks, pieces * 2 * share, LANES)
    gathered = lax.all_to_all(packed, "ctx", split_axis=0, concat_axis=0, tiled=True)
    gathered = gathered.reshape(rows * 2 * share, LANES)
    tables = transform_tables(rows, LANES)
    conv = pl.pallas_call(
        functools.partial(conv_kernel, 4, share),
        out_shape=jax.ShapeDtypeStruct((rows * share, LANES), F32),
        compiler_params=params,
        name="conv",
    )(gathered, *tables)
    conv = conv.reshape(blocks, pieces * share, LANES)
    conv = lax.all_to_all(conv, "ctx", split_axis=0, concat_axis=0, tiled=True)
    conv = conv.reshape(blocks, pieces, share, LANES)
    gated, square = pl.pallas_call(
        gate_kernel,
        out_shape=[
            jax.ShapeDtypeStruct((tokens, channels), F32),
            jax.ShapeDtypeStruct((peers, tokens), F32),
        ],
        compiler_params=params,
        name="gate",
    )(conv, query_gate, key_branch, value_branch, skip_weight[None])
    square = lax.all_to_all(square, "chan", split_axis=0, concat_axis=0, tiled=True)
    return pl.pallas_call(
        norm_kernel,
        out_shape=jax.ShapeDtypeStruct((tokens, channels), BF16),
        compiler_params=params,
        name="norm",
    )(gated, square, norm_gain[None])


def solution(mesh):
    wide = P("ctx", "chan")
    return jax.shard_map(
        on_device,
        mesh=mesh,
        in_specs=(wide, wide, wide, wide, P("chan"), P("chan")),
        out_specs=wide,
        check_vma=False,
    )
```

```python
import functools
import math

import jax
import jax.numpy as jnp
import ml_dtypes
import numpy as np
from jax import lax
from jax.experimental import pallas as pl
from jax.experimental.pallas import tpu as pltpu
from jax.sharding import PartitionSpec as P

CH = 4096
LANES = 128
F32 = jnp.float32
BF16 = jnp.bfloat16
VMEM_BYTES = 32 * 1024 * 1024


def split_const(values):
    high = values.astype(ml_dtypes.bfloat16)
    low = (values - high.astype(np.float64)).astype(ml_dtypes.bfloat16)
    return high, low


def transform_tables(rows, cols):
    length = rows * cols
    m = np.arange(rows, dtype=np.float64)
    b = np.arange(cols, dtype=np.float64)
    first = 2.0 * math.pi * np.outer(m + 0.25, m) / rows
    first_high, first_low = split_const(np.concatenate([np.cos(first), -np.sin(first)], axis=0))
    first_table = np.block([[first_high, first_high], [first_low, np.zeros_like(first_low)]])
    turn = 2.0 * math.pi * np.outer(m + 0.25, b) / length
    turn_re = np.cos(turn).astype(np.float32)
    turn_im = (-np.sin(turn)).astype(np.float32)
    second = 2.0 * math.pi * (np.outer(b, b) % cols) / cols
    cosine, sine = np.cos(second), np.sin(second)
    fwd_high, fwd_low = split_const(np.block([[cosine, -sine], [sine, cosine]]))
    fwd_table = np.concatenate([fwd_high, fwd_high, fwd_low], axis=0)
    back_high, back_low = split_const(np.block([[cosine, sine], [-sine, cosine]]))
    back_table = np.concatenate([back_high, back_high, back_low], axis=0)
    last_high, last_low = split_const(
        np.concatenate([np.cos(first.T), -np.sin(first.T)], axis=1) / length
    )
    last_table = np.concatenate([last_high, last_low], axis=0)
    return first_table, turn_re, turn_im, fwd_table, back_table, last_table


def split(values):
    high = values.astype(BF16)
    low = (values - high.astype(F32)).astype(BF16)
    return high, low


def dot(left, right):
    return jnp.dot(left, right, preferred_element_type=F32)


def pack_kernel(key_hbm, value_hbm, filter_hbm, out_ref, key_ref, value_ref, filter_ref, sems):
    pieces, share = out_ref.shape[1], out_ref.shape[3]
    half = pieces // 2
    pairs = ((key_hbm, key_ref), (value_hbm, value_ref), (filter_hbm, filter_ref))
    copies = []
    for part in range(2):
        at = pl.ds(part * half * LANES, half * LANES)
        for index, (source, target) in enumerate(pairs):
            copies.append(
                pltpu.make_async_copy(source.at[at], target.at[at], sems.at[part, index])
            )
    for copy in copies:
        copy.start()
    for piece in range(pieces):
        at = pl.ds(piece * LANES, LANES)
        if piece % half == 0:
            copies[3 * (piece // half)].wait()
            copies[3 * (piece // half) + 1].wait()
        product = key_ref[at, :].astype(F32) * value_ref[at, :].astype(F32)
        out_ref[:, piece, 0] = product.T.reshape(-1, share, LANES)
        if piece % half == 0:
            copies[3 * (piece // half) + 2].wait()
        out_ref[:, piece, 1] = filter_ref[at, :].T.reshape(-1, share, LANES)


def conv_kernel(
    group, share, data_ref, first_ref, turn_re_ref, turn_im_ref, fwd_ref, back_ref, last_ref, out_ref
):
    rows = turn_re_ref.shape[0]
    turn_re = jnp.concatenate([turn_re_ref[...]] * 2, axis=1)
    turn_im = jnp.concatenate([turn_im_ref[...]] * 2, axis=1)

    def over_lanes(values, table_ref):
        high, low = split(values)
        return dot(jnp.concatenate([high, low, high], axis=1), table_ref[...])

    def first_stage(start):
        parts = []
        for c in range(start, start + group):
            signal = data_ref[pl.ds(c, rows, stride=2 * share), :]
            kernel = data_ref[pl.ds(share + c, rows, stride=2 * share), :]
            high, low = split(jnp.concatenate([signal, kernel], axis=1))
            spec = dot(first_ref[...], jnp.concatenate([high, low], axis=0))
            re = spec[:rows] + spec[2 * rows : 3 * rows]
            im = spec[rows : 2 * rows] + spec[3 * rows :]
            out_re = re * turn_re - im * turn_im
            out_im = re * turn_im + im * turn_re
            parts.append(jnp.concatenate([out_re[:, :LANES], out_im[:, :LANES]], axis=1))
            parts.append(jnp.concatenate([out_re[:, LANES:], out_im[:, LANES:]], axis=1))
        return jnp.concatenate(parts, axis=0)

    def product_of_spectra(turned):
        spec = over_lanes(turned, fwd_ref)
        parts = []
        for c in range(group):
            signal = spec[2 * c * rows : (2 * c + 1) * rows]
            kernel = spec[(2 * c + 1) * rows : (2 * c + 2) * rows]
            s_re, s_im = signal[:, :LANES], signal[:, LANES:]
            k_re, k_im = kernel[:, :LANES], kernel[:, LANES:]
            parts.append(
                jnp.concatenate([s_re * k_re - s_im * k_im, s_re * k_im + s_im * k_re], axis=1)
            )
        return jnp.concatenate(parts, axis=0)

    def last_stage(spec, start):
        for c in range(0, group, 2):
            first = spec[c * rows : (c + 1) * rows]
            second = spec[(c + 1) * rows : (c + 2) * rows]
            re = jnp.concatenate([first[:, :LANES], second[:, :LANES]], axis=1)
            im = jnp.concatenate([first[:, LANES:], second[:, LANES:]], axis=1)
            turned = jnp.concatenate(
                [re * turn_re + im * turn_im, im * turn_re - re * turn_im], axis=0
            )
            high, low = split(turned)
            conv = dot(last_ref[...], high)
            conv = conv[:rows] + dot(last_ref[:rows], low) + conv[rows:]
            out_ref[pl.ds(start + c, rows, stride=share), :] = conv[:, :LANES]
            out_ref[pl.ds(start + c + 1, rows, stride=share), :] = conv[:, LANES:]

    groups = share // group
    turned, spectra, back = {}, {}, {}
    for step in range(groups + 3):
        if 0 <= step - 1 < groups:
            spectra[step - 1] = product_of_spectra(turned.pop(step - 1))
        if step < groups:
            turned[step] = first_stage(step * group)
        if 0 <= step - 3 < groups:
            last_stage(back.pop(step - 3), (step - 3) * group)
        if 0 <= step - 2 < groups:
            back[step - 2] = over_lanes(spectra.pop(step - 2), back_ref)


def gate_kernel(conv_ref, query_ref, key_ref, value_ref, skip_ref, gated_ref, square_ref):
    for piece in range(conv_ref.shape[1]):
        at = slice(piece * LANES, (piece + 1) * LANES)
        conv = conv_ref[:, piece].reshape(-1, LANES).T
        product = key_ref[at, :].astype(F32) * value_ref[at, :].astype(F32)
        gated = query_ref[at, :].astype(F32) * (conv + skip_ref[...] * product)
        gated_ref[at, :] = gated
        square = gated * gated
        folded = square[:, :LANES]
        for start in range(LANES, square.shape[1], LANES):
            folded = folded + square[:, start : start + LANES]
        total = jnp.sum(folded.T, axis=0, keepdims=True)
        square_ref[:, at] = jnp.broadcast_to(total, (square_ref.shape[0], LANES))


def norm_kernel(gated_ref, square_ref, gain_ref, out_ref):
    total = jnp.sum(square_ref[...], axis=0, keepdims=True)
    inverse = lax.rsqrt(total / CH + 1e-05)
    for top in range(0, out_ref.shape[0], LANES):
        down = slice(top, top + LANES)
        spread = jnp.broadcast_to(inverse[:, down], (LANES, LANES)).T
        for start in range(0, out_ref.shape[1], LANES):
            at = slice(start, start + LANES)
            out_ref[down, at] = (gated_ref[down, at] * spread * gain_ref[:, at]).astype(BF16)


def on_device(query_gate, key_branch, value_branch, conv_filter, skip_weight, norm_gain):
    blocks = lax.axis_size("ctx")
    peers = lax.axis_size("chan")
    tokens, channels = key_branch.shape
    share = channels // blocks
    pieces = tokens // LANES
    rows = blocks * pieces
    params = pltpu.CompilerParams(vmem_limit_bytes=VMEM_BYTES)
    strip = pl.BlockSpec((LANES, channels), lambda a: (a, 0))
    row = pl.BlockSpec((1, channels), lambda a: (0, 0))
    whole = (tokens, channels)
    whole = (tokens, channels)
    packed_shape = (blocks, pieces, 2, share, LANES)
    inputs = [
        pltpu.with_memory_space_constraint(array, pltpu.HBM)
        for array in (key_branch, value_branch, conv_filter)
    ]
    packed = pl.pallas_call(
        pack_kernel,
        in_specs=[pl.BlockSpec(memory_space=pltpu.HBM)] * 3,
        out_specs=pl.BlockSpec(memory_space=pltpu.VMEM),
        out_shape=jax.ShapeDtypeStruct(packed_shape, F32),
        scratch_shapes=[
            pltpu.VMEM(whole, BF16),
            pltpu.VMEM(whole, BF16),
            pltpu.VMEM(whole, F32),
            pltpu.SemaphoreType.DMA((2, 3)),
        ],
        compiler_params=params,
        name="pack",
    )(*inputs)
    packed = packed.reshape(blocks, pieces * 2 * share, LANES)
    gathered = lax.all_to_all(packed, "ctx", split_axis=0, concat_axis=0, tiled=True)
    gathered = gathered.reshape(rows * 2 * share, LANES)
    tables = transform_tables(rows, LANES)
    conv = pl.pallas_call(
        functools.partial(conv_kernel, 4, share),
        out_shape=jax.ShapeDtypeStruct((rows * share, LANES), F32),
        compiler_params=params,
        name="conv",
    )(gathered, *tables)
    conv = conv.reshape(blocks, pieces * share, LANES)
    conv = lax.all_to_all(conv, "ctx", split_axis=0, concat_axis=0, tiled=True)
    conv = conv.reshape(blocks, pieces, share, LANES)
    gated, square = pl.pallas_call(
        gate_kernel,
        out_shape=[
            jax.ShapeDtypeStruct((tokens, channels), F32),
            jax.ShapeDtypeStruct((peers, tokens), F32),
        ],
        compiler_params=params,
        name="gate",
    )(conv, query_gate, key_branch, value_branch, skip_weight[None])
    square = lax.all_to_all(square, "chan", split_axis=0, concat_axis=0, tiled=True)
    return pl.pallas_call(
        norm_kernel,
        out_shape=jax.ShapeDtypeStruct((tokens, channels), BF16),
        compiler_params=params,
        name="norm",
    )(gated, square, norm_gain[None])


def solution(mesh):
    wide = P("ctx", "chan")
    return jax.shard_map(
        on_device,
        mesh=mesh,
        in_specs=(wide, wide, wide, wide, P("chan"), P("chan")),
        out_specs=wide,
        check_vma=False,
    )
```

```python
import functools
import math

import jax
import jax.numpy as jnp
import ml_dtypes
import numpy as np
from jax import lax
from jax.experimental import pallas as pl
from jax.experimental.pallas import tpu as pltpu
from jax.sharding import PartitionSpec as P

CH = 4096
LANES = 128
F32 = jnp.float32
BF16 = jnp.bfloat16
VMEM_BYTES = 32 * 1024 * 1024


def split_const(values):
    high = values.astype(ml_dtypes.bfloat16)
    low = (values - high.astype(np.float64)).astype(ml_dtypes.bfloat16)
    return high, low


def transform_tables(rows, cols):
    length = rows * cols
    m = np.arange(rows, dtype=np.float64)
    b = np.arange(cols, dtype=np.float64)
    first = 2.0 * math.pi * np.outer(m + 0.25, m) / rows
    first_parts = []
    for parity in range(2):
        angle = first[: rows // 2, parity::2]
        high, low = split_const(np.concatenate([np.cos(angle), -np.sin(angle)], axis=0))
        first_parts.append(np.concatenate([high, high, low], axis=1))
    first_table = np.concatenate(first_parts, axis=0)
    turn = 2.0 * math.pi * np.outer(m + 0.25, b) / length
    turn_re = np.cos(turn).astype(np.float32)
    turn_im = (-np.sin(turn)).astype(np.float32)
    second = 2.0 * math.pi * (np.outer(b, b) % cols) / cols
    cosine, sine = np.cos(second), np.sin(second)
    fwd_high, fwd_low = split_const(np.block([[cosine, -sine], [sine, cosine]]))
    fwd_table = np.concatenate([fwd_high, fwd_high, fwd_low], axis=0)
    back_high, back_low = split_const(np.block([[cosine, sine], [-sine, cosine]]))
    back_table = np.concatenate([back_high, back_high, back_low], axis=0)
    last_high, last_low = split_const(
        np.concatenate([np.cos(first.T), -np.sin(first.T)], axis=1) / length
    )
    last_table = np.concatenate([last_high, last_low], axis=0)
    return first_table, turn_re, turn_im, fwd_table, back_table, last_table


def split(values):
    high = values.astype(BF16)
    low = (values - high.astype(F32)).astype(BF16)
    return high, low


def dot(left, right):
    return jnp.dot(left, right, preferred_element_type=F32)


def pack_kernel(key_hbm, value_hbm, filter_hbm, out_ref, key_ref, value_ref, filter_ref, sems):
    pieces, share = out_ref.shape[1], out_ref.shape[3]
    half = pieces // 2
    pairs = ((key_hbm, key_ref), (value_hbm, value_ref), (filter_hbm, filter_ref))
    copies = []
    for part in range(2):
        at = pl.ds(part * half * LANES, half * LANES)
        for index, (source, target) in enumerate(pairs):
            copies.append(
                pltpu.make_async_copy(source.at[at], target.at[at], sems.at[part, index])
            )
    for copy in copies:
        copy.start()
    for piece in range(pieces):
        at = pl.ds(piece * LANES, LANES)
        if piece % half == 0:
            copies[3 * (piece // half)].wait()
            copies[3 * (piece // half) + 1].wait()
        product = key_ref[at, :].astype(F32) * value_ref[at, :].astype(F32)
        out_ref[:, piece, 0] = product.T.reshape(-1, share, LANES)
        if piece % half == 0:
            copies[3 * (piece // half) + 2].wait()
        out_ref[:, piece, 1] = filter_ref[at, :].T.reshape(-1, share, LANES)


def conv_kernel(
    group, share, data_ref, first_ref, turn_re_ref, turn_im_ref, fwd_ref, back_ref, last_ref, out_ref
):
    rows = turn_re_ref.shape[0]
    half = rows // 2
    turn_re = jnp.concatenate([turn_re_ref[...]] * 2, axis=1)
    turn_im = jnp.concatenate([turn_im_ref[...]] * 2, axis=1)

    def over_lanes(values, table_ref):
        high, low = split(values)
        return dot(jnp.concatenate([high, low, high], axis=1), table_ref[...])

    def half_sum(start, parity):
        signal = data_ref[pl.ds(2 * share * parity + start, half, stride=4 * share), :]
        kernel = data_ref[pl.ds(2 * share * parity + share + start, half, stride=4 * share), :]
        high, low = split(jnp.concatenate([signal, kernel], axis=1))
        table = first_ref[rows * parity : rows * (parity + 1)]
        return dot(table, jnp.concatenate([high, low, high], axis=0))

    def first_stage(start):
        parts = []
        for c in range(start, start + group):
            even, odd = half_sum(c, 0), half_sum(c, 1)
            total, difference = even + odd, even - odd
            re = jnp.concatenate([total[:half], difference[:half]], axis=0)
            im = jnp.concatenate([total[half:], difference[half:]], axis=0)
            out_re = re * turn_re - im * turn_im
            out_im = re * turn_im + im * turn_re
            parts.append(jnp.concatenate([out_re[:, :LANES], out_im[:, :LANES]], axis=1))
            parts.append(jnp.concatenate([out_re[:, LANES:], out_im[:, LANES:]], axis=1))
        return jnp.concatenate(parts, axis=0)

    def product_of_spectra(turned):
        spec = over_lanes(turned, fwd_ref)
        parts = []
        for c in range(group):
            signal = spec[2 * c * rows : (2 * c + 1) * rows]
            kernel = spec[(2 * c + 1) * rows : (2 * c + 2) * rows]
            s_re, s_im = signal[:, :LANES], signal[:, LANES:]
            k_re, k_im = kernel[:, :LANES], kernel[:, LANES:]
            parts.append(
                jnp.concatenate([s_re * k_re - s_im * k_im, s_re * k_im + s_im * k_re], axis=1)
            )
        return jnp.concatenate(parts, axis=0)

    def last_stage(spec, start):
        for c in range(0, group, 2):
            first = spec[c * rows : (c + 1) * rows]
            second = spec[(c + 1) * rows : (c + 2) * rows]
            re = jnp.concatenate([first[:, :LANES], second[:, :LANES]], axis=1)
            im = jnp.concatenate([first[:, LANES:], second[:, LANES:]], axis=1)
            turned = jnp.concatenate(
                [re * turn_re + im * turn_im, im * turn_re - re * turn_im], axis=0
            )
            high, low = split(turned)
            conv = dot(last_ref[...], high)
            conv = conv[:rows] + dot(last_ref[:rows], low) + conv[rows:]
            out_ref[pl.ds(start + c, rows, stride=share), :] = conv[:, :LANES]
            out_ref[pl.ds(start + c + 1, rows, stride=share), :] = conv[:, LANES:]

    groups = share // group
    turned, spectra, back = {}, {}, {}
    for step in range(groups + 3):
        if step < groups:
            turned[step] = first_stage(step * group)
        if 0 <= step - 1 < groups:
            spectra[step - 1] = product_of_spectra(turned.pop(step - 1))
        if 0 <= step - 2 < groups:
            back[step - 2] = over_lanes(spectra.pop(step - 2), back_ref)
        if 0 <= step - 3 < groups:
            last_stage(back.pop(step - 3), (step - 3) * group)


def gate_kernel(conv_ref, query_ref, key_ref, value_ref, skip_ref, gated_ref, square_ref):
    for piece in range(conv_ref.shape[1]):
        at = slice(piece * LANES, (piece + 1) * LANES)
        conv = conv_ref[:, piece].reshape(-1, LANES).T
        product = key_ref[at, :].astype(F32) * value_ref[at, :].astype(F32)
        gated = query_ref[at, :].astype(F32) * (conv + skip_ref[...] * product)
        gated_ref[at, :] = gated
        square = gated * gated
        folded = square[:, :LANES]
        for start in range(LANES, square.shape[1], LANES):
            folded = folded + square[:, start : start + LANES]
        total = jnp.sum(folded.T, axis=0, keepdims=True)
        square_ref[:, at] = jnp.broadcast_to(total, (square_ref.shape[0], LANES))


def norm_kernel(gated_ref, square_ref, gain_ref, out_hbm, out_ref, sems):
    total = jnp.sum(square_ref[...], axis=0, keepdims=True)
    inverse = lax.rsqrt(total / CH + 1e-05)
    half = out_ref.shape[0] // 2
    sends = []
    for top in range(0, out_ref.shape[0], LANES):
        down = slice(top, top + LANES)
        spread = jnp.broadcast_to(inverse[:, down], (LANES, LANES)).T
        for start in range(0, out_ref.shape[1], LANES):
            at = slice(start, start + LANES)
            out_ref[down, at] = (gated_ref[down, at] * spread * gain_ref[:, at]).astype(BF16)
        if (top + LANES) % half == 0:
            part = pl.ds(top + LANES - half, half)
            sends.append(
                pltpu.make_async_copy(out_ref.at[part], out_hbm.at[part], sems.at[len(sends)])
            )
            sends[-1].start()
    for copy in sends:
        copy.wait()


def on_device(query_gate, key_branch, value_branch, conv_filter, skip_weight, norm_gain):
    blocks = lax.axis_size("ctx")
    peers = lax.axis_size("chan")
    tokens, channels = key_branch.shape
    share = channels // blocks
    pieces = tokens // LANES
    rows = blocks * pieces
    params = pltpu.CompilerParams(vmem_limit_bytes=VMEM_BYTES)
    strip = pl.BlockSpec((LANES, channels), lambda a: (a, 0))
    row = pl.BlockSpec((1, channels), lambda a: (0, 0))
    whole = (tokens, channels)
    packed_shape = (blocks, pieces, 2, share, LANES)
    inputs = [
        pltpu.with_memory_space_constraint(array, pltpu.HBM)
        for array in (key_branch, value_branch, conv_filter)
    ]
    packed = pl.pallas_call(
        pack_kernel,
        in_specs=[pl.BlockSpec(memory_space=pltpu.HBM)] * 3,
        out_specs=pl.BlockSpec(memory_space=pltpu.VMEM),
        out_shape=jax.ShapeDtypeStruct(packed_shape, F32),
        scratch_shapes=[
            pltpu.VMEM(whole, BF16),
            pltpu.VMEM(whole, BF16),
            pltpu.VMEM(whole, F32),
            pltpu.SemaphoreType.DMA((2, 3)),
        ],
        compiler_params=params,
        name="pack",
    )(*inputs)
    packed = packed.reshape(blocks, pieces * 2 * share, LANES)
    gathered = lax.all_to_all(packed, "ctx", split_axis=0, concat_axis=0, tiled=True)
    gathered = gathered.reshape(rows * 2 * share, LANES)
    tables = transform_tables(rows, LANES)
    conv = pl.pallas_call(
        functools.partial(conv_kernel, 2, share),
        out_shape=jax.ShapeDtypeStruct((rows * share, LANES), F32),
        compiler_params=params,
        name="conv",
    )(gathered, *tables)
    conv = conv.reshape(blocks, pieces * share, LANES)
    conv = lax.all_to_all(conv, "ctx", split_axis=0, concat_axis=0, tiled=True)
    conv = conv.reshape(blocks, pieces, share, LANES)
    gated, square = pl.pallas_call(
        gate_kernel,
        out_shape=[
            jax.ShapeDtypeStruct((tokens, channels), F32),
            jax.ShapeDtypeStruct((peers, tokens), F32),
        ],
        compiler_params=params,
        name="gate",
    )(conv, query_gate, key_branch, value_branch, skip_weight[None])
    square = lax.all_to_all(square, "chan", split_axis=0, concat_axis=0, tiled=True)
    return pl.pallas_call(
        norm_kernel,
        in_specs=[pl.BlockSpec(memory_space=pltpu.VMEM)] * 3,
        out_specs=pl.BlockSpec(memory_space=pltpu.HBM),
        out_shape=jax.ShapeDtypeStruct(whole, BF16),
        scratch_shapes=[pltpu.VMEM(whole, BF16), pltpu.SemaphoreType.DMA((2,))],
        compiler_params=params,
        name="norm",
    )(gated, square, norm_gain[None])


def solution(mesh):
    wide = P("ctx", "chan")
    return jax.shard_map(
        on_device,
        mesh=mesh,
        in_specs=(wide, wide, wide, wide, P("chan"), P("chan")),
        out_specs=wide,
        check_vma=False,
    )
```

```python
import functools
import math

import jax
import jax.numpy as jnp
import ml_dtypes
import numpy as np
from jax import lax
from jax.experimental import pallas as pl
from jax.experimental.pallas import tpu as pltpu
from jax.sharding import PartitionSpec as P

CH = 4096
LANES = 128
F32 = jnp.float32
BF16 = jnp.bfloat16
VMEM_BYTES = 32 * 1024 * 1024


def split_const(values):
    high = values.astype(ml_dtypes.bfloat16)
    low = (values - high.astype(np.float64)).astype(ml_dtypes.bfloat16)
    return high, low


def transform_tables(rows, cols):
    length = rows * cols
    m = np.arange(rows, dtype=np.float64)
    b = np.arange(cols, dtype=np.float64)
    first = 2.0 * math.pi * np.outer(m + 0.25, m) / rows
    first_parts = []
    for parity in range(2):
        angle = first[: rows // 2, parity::2]
        high, low = split_const(np.concatenate([np.cos(angle), -np.sin(angle)], axis=0))
        first_parts.append(np.concatenate([high, high, low], axis=1))
    first_table = np.concatenate(first_parts, axis=0)
    turn = 2.0 * math.pi * np.outer(m + 0.25, b) / length
    turn_re = np.cos(turn).astype(np.float32)
    turn_im = (-np.sin(turn)).astype(np.float32)
    second = 2.0 * math.pi * (np.outer(b, b) % cols) / cols
    cosine, sine = np.cos(second), np.sin(second)
    fwd_high, fwd_low = split_const(np.block([[cosine, -sine], [sine, cosine]]))
    fwd_table = np.concatenate([fwd_high, fwd_high, fwd_low], axis=0)
    back_high, back_low = split_const(np.block([[cosine, sine], [-sine, cosine]]))
    back_table = np.concatenate([back_high, back_high, back_low], axis=0)
    last_high, last_low = split_const(
        np.concatenate([np.cos(first.T), -np.sin(first.T)], axis=1) / length
    )
    last_table = np.concatenate([last_high, last_low], axis=0)
    return first_table, turn_re, turn_im, fwd_table, back_table, last_table


def split(values):
    high = values.astype(BF16)
    low = (values - high.astype(F32)).astype(BF16)
    return high, low


def dot(left, right):
    return jnp.dot(left, right, preferred_element_type=F32)


def pack_kernel(key_hbm, value_hbm, filter_hbm, out_ref, key_ref, value_ref, filter_ref, sems):
    pieces, share = out_ref.shape[1], out_ref.shape[3]
    half = pieces // 2
    pairs = ((key_hbm, key_ref), (value_hbm, value_ref), (filter_hbm, filter_ref))
    copies = []
    for part in range(2):
        at = pl.ds(part * half * LANES, half * LANES)
        for index, (source, target) in enumerate(pairs):
            copies.append(
                pltpu.make_async_copy(source.at[at], target.at[at], sems.at[part, index])
            )
    for copy in copies:
        copy.start()
    for piece in range(pieces):
        at = pl.ds(piece * LANES, LANES)
        if piece % half == 0:
            copies[3 * (piece // half)].wait()
            copies[3 * (piece // half) + 1].wait()
        product = key_ref[at, :].astype(F32) * value_ref[at, :].astype(F32)
        out_ref[:, piece, 0] = product.T.reshape(-1, share, LANES)
        if piece % half == 0:
            copies[3 * (piece // half) + 2].wait()
        out_ref[:, piece, 1] = filter_ref[at, :].T.reshape(-1, share, LANES)


def conv_kernel(
    group, share, data_ref, first_ref, turn_re_ref, turn_im_ref, fwd_ref, back_ref, last_ref, out_ref
):
    rows = turn_re_ref.shape[0]
    half = rows // 2
    turn_re = jnp.concatenate([turn_re_ref[...]] * 2, axis=1)
    turn_im = jnp.concatenate([turn_im_ref[...]] * 2, axis=1)

    def over_lanes(values, table_ref):
        high, low = split(values)
        return dot(jnp.concatenate([high, low, high], axis=1), table_ref[...])

    def half_sum(start, parity):
        signal = data_ref[pl.ds(2 * share * parity + start, half, stride=4 * share), :]
        kernel = data_ref[pl.ds(2 * share * parity + share + start, half, stride=4 * share), :]
        high, low = split(jnp.concatenate([signal, kernel], axis=1))
        table = first_ref[rows * parity : rows * (parity + 1)]
        return dot(table, jnp.concatenate([high, low, high], axis=0))

    def first_stage(start):
        parts = []
        for c in range(start, start + group):
            even, odd = half_sum(c, 0), half_sum(c, 1)
            total, difference = even + odd, even - odd
            re = jnp.concatenate([total[:half], difference[:half]], axis=0)
            im = jnp.concatenate([total[half:], difference[half:]], axis=0)
            out_re = re * turn_re - im * turn_im
            out_im = re * turn_im + im * turn_re
            parts.append(jnp.concatenate([out_re[:, :LANES], out_im[:, :LANES]], axis=1))
            parts.append(jnp.concatenate([out_re[:, LANES:], out_im[:, LANES:]], axis=1))
        return jnp.concatenate(parts, axis=0)

    def product_of_spectra(turned):
        spec = over_lanes(turned, fwd_ref)
        parts = []
        for c in range(group):
            signal = spec[2 * c * rows : (2 * c + 1) * rows]
            kernel = spec[(2 * c + 1) * rows : (2 * c + 2) * rows]
            s_re, s_im = signal[:, :LANES], signal[:, LANES:]
            k_re, k_im = kernel[:, :LANES], kernel[:, LANES:]
            parts.append(
                jnp.concatenate([s_re * k_re - s_im * k_im, s_re * k_im + s_im * k_re], axis=1)
            )
        return jnp.concatenate(parts, axis=0)

    def last_stage(spec, start):
        for c in range(0, group, 2):
            first = spec[c * rows : (c + 1) * rows]
            second = spec[(c + 1) * rows : (c + 2) * rows]
            re = jnp.concatenate([first[:, :LANES], second[:, :LANES]], axis=1)
            im = jnp.concatenate([first[:, LANES:], second[:, LANES:]], axis=1)
            turned = jnp.concatenate(
                [re * turn_re + im * turn_im, im * turn_re - re * turn_im], axis=0
            )
            high, low = split(turned)
            conv = dot(last_ref[...], high)
            conv = conv[:rows] + dot(last_ref[:rows], low) + conv[rows:]
            out_ref[pl.ds(start + c, rows, stride=share), :] = conv[:, :LANES]
            out_ref[pl.ds(start + c + 1, rows, stride=share), :] = conv[:, LANES:]

    groups = share // group
    turned, spectra, back = {}, {}, {}
    for step in range(groups + 3):
        if step < groups:
            turned[step] = first_stage(step * group)
        if 0 <= step - 1 < groups:
            spectra[step - 1] = product_of_spectra(turned.pop(step - 1))
        if 0 <= step - 2 < groups:
            back[step - 2] = over_lanes(spectra.pop(step - 2), back_ref)
        if 0 <= step - 3 < groups:
            last_stage(back.pop(step - 3), (step - 3) * group)


def gate_kernel(
    conv_ref, query_ref, key_ref, value_ref, skip_ref, gain_ref, gated_ref, square_ref
):
    for piece in range(conv_ref.shape[1]):
        at = slice(piece * LANES, (piece + 1) * LANES)
        conv = conv_ref[:, piece].reshape(-1, LANES).T
        product = key_ref[at, :].astype(F32) * value_ref[at, :].astype(F32)
        gated = query_ref[at, :].astype(F32) * (conv + skip_ref[...] * product)
        gated_ref[at, :] = gated * gain_ref[...]
        square = gated * gated
        folded = square[:, :LANES]
        for start in range(LANES, square.shape[1], LANES):
            folded = folded + square[:, start : start + LANES]
        total = jnp.sum(folded.T, axis=0, keepdims=True)
        square_ref[:, at] = jnp.broadcast_to(total, (square_ref.shape[0], LANES))


def norm_kernel(gated_ref, square_ref, out_hbm, out_ref, sems):
    total = jnp.sum(square_ref[...], axis=0, keepdims=True)
    inverse = lax.rsqrt(total / CH + 1e-05)
    part_rows = out_ref.shape[0] // 4
    sends = []
    for top in range(0, out_ref.shape[0], LANES):
        down = slice(top, top + LANES)
        spread = jnp.broadcast_to(inverse[:, down], (LANES, LANES)).T
        for start in range(0, out_ref.shape[1], LANES):
            at = slice(start, start + LANES)
            out_ref[down, at] = (gated_ref[down, at] * spread).astype(BF16)
        if (top + LANES) % part_rows == 0:
            part = pl.ds(top + LANES - part_rows, part_rows)
            sends.append(
                pltpu.make_async_copy(out_ref.at[part], out_hbm.at[part], sems.at[len(sends)])
            )
            sends[-1].start()
    for copy in sends:
        copy.wait()


def on_device(query_gate, key_branch, value_branch, conv_filter, skip_weight, norm_gain):
    blocks = lax.axis_size("ctx")
    peers = lax.axis_size("chan")
    tokens, channels = key_branch.shape
    share = channels // blocks
    pieces = tokens // LANES
    rows = blocks * pieces
    params = pltpu.CompilerParams(vmem_limit_bytes=VMEM_BYTES)
    strip = pl.BlockSpec((LANES, channels), lambda a: (a, 0))
    row = pl.BlockSpec((1, channels), lambda a: (0, 0))
    whole = (tokens, channels)
    packed_shape = (blocks, pieces, 2, share, LANES)
    inputs = [
        pltpu.with_memory_space_constraint(array, pltpu.HBM)
        for array in (key_branch, value_branch, conv_filter)
    ]
    packed = pl.pallas_call(
        pack_kernel,
        in_specs=[pl.BlockSpec(memory_space=pltpu.HBM)] * 3,
        out_specs=pl.BlockSpec(memory_space=pltpu.VMEM),
        out_shape=jax.ShapeDtypeStruct(packed_shape, F32),
        scratch_shapes=[
            pltpu.VMEM(whole, BF16),
            pltpu.VMEM(whole, BF16),
            pltpu.VMEM(whole, F32),
            pltpu.SemaphoreType.DMA((2, 3)),
        ],
        compiler_params=params,
        name="pack",
    )(*inputs)
    packed = packed.reshape(blocks, pieces * 2 * share, LANES)
    gathered = lax.all_to_all(packed, "ctx", split_axis=0, concat_axis=0, tiled=True)
    gathered = gathered.reshape(rows * 2 * share, LANES)
    tables = transform_tables(rows, LANES)
    conv = pl.pallas_call(
        functools.partial(conv_kernel, 2, share),
        out_shape=jax.ShapeDtypeStruct((rows * share, LANES), F32),
        compiler_params=params,
        name="conv",
    )(gathered, *tables)
    conv = conv.reshape(blocks, pieces * share, LANES)
    conv = lax.all_to_all(conv, "ctx", split_axis=0, concat_axis=0, tiled=True)
    conv = conv.reshape(blocks, pieces, share, LANES)
    gated, square = pl.pallas_call(
        gate_kernel,
        out_shape=[
            jax.ShapeDtypeStruct((tokens, channels), F32),
            jax.ShapeDtypeStruct((peers, tokens), F32),
        ],
        compiler_params=params,
        name="gate",
    )(conv, query_gate, key_branch, value_branch, skip_weight[None], norm_gain[None])
    square = lax.all_to_all(square, "chan", split_axis=0, concat_axis=0, tiled=True)
    return pl.pallas_call(
        norm_kernel,
        in_specs=[pl.BlockSpec(memory_space=pltpu.VMEM)] * 2,
        out_specs=pl.BlockSpec(memory_space=pltpu.HBM),
        out_shape=jax.ShapeDtypeStruct(whole, BF16),
        scratch_shapes=[pltpu.VMEM(whole, BF16), pltpu.SemaphoreType.DMA((4,))],
        compiler_params=params,
        name="norm",
    )(gated, square)


def solution(mesh):
    wide = P("ctx", "chan")
    return jax.shard_map(
        on_device,
        mesh=mesh,
        in_specs=(wide, wide, wide, wide, P("chan"), P("chan")),
        out_specs=wide,
        check_vma=False,
    )
```

```python
import functools
import math

import jax
import jax.numpy as jnp
import ml_dtypes
import numpy as np
from jax import lax
from jax.experimental import pallas as pl
from jax.experimental.pallas import tpu as pltpu
from jax.sharding import PartitionSpec as P

CH = 4096
LANES = 128
F32 = jnp.float32
BF16 = jnp.bfloat16
VMEM_BYTES = 32 * 1024 * 1024


def split_const(values):
    high = values.astype(ml_dtypes.bfloat16)
    low = (values - high.astype(np.float64)).astype(ml_dtypes.bfloat16)
    return high, low


def transform_tables(rows, cols):
    length = rows * cols
    m = np.arange(rows, dtype=np.float64)
    b = np.arange(cols, dtype=np.float64)
    first = 2.0 * math.pi * np.outer(m + 0.25, m) / rows
    first_parts = []
    for parity in range(2):
        angle = first[: rows // 2, parity::2]
        high, low = split_const(np.concatenate([np.cos(angle), -np.sin(angle)], axis=0))
        first_parts.append(np.concatenate([high, high, low], axis=1))
    first_table = np.concatenate(first_parts, axis=0)
    turn = 2.0 * math.pi * np.outer(m + 0.25, b) / length
    turn_re = np.cos(turn).astype(np.float32)
    turn_im = (-np.sin(turn)).astype(np.float32)
    second = 2.0 * math.pi * (np.outer(b, b) % cols) / cols
    cosine, sine = np.cos(second), np.sin(second)
    fwd_high, fwd_low = split_const(np.block([[cosine, -sine], [sine, cosine]]))
    fwd_table = np.concatenate([fwd_high, fwd_high, fwd_low], axis=0)
    back_high, back_low = split_const(np.block([[cosine, sine], [-sine, cosine]]))
    back_table = np.concatenate([back_high, back_high, back_low], axis=0)
    last_high, last_low = split_const(
        np.concatenate([np.cos(first.T), -np.sin(first.T)], axis=1) / length
    )
    last_table = np.concatenate([last_high, last_low], axis=0)
    return first_table, turn_re, turn_im, fwd_table, back_table, last_table


def split(values):
    high = values.astype(BF16)
    low = (values - high.astype(F32)).astype(BF16)
    return high, low


def dot(left, right):
    return jnp.dot(left, right, preferred_element_type=F32)


def pack_kernel(key_hbm, value_hbm, filter_hbm, out_ref, key_ref, value_ref, filter_ref, sems):
    pieces, share = out_ref.shape[1], out_ref.shape[3]
    half = pieces // 2
    pairs = ((key_hbm, key_ref), (value_hbm, value_ref), (filter_hbm, filter_ref))
    copies = []
    for part in range(2):
        at = pl.ds(part * half * LANES, half * LANES)
        for index, (source, target) in enumerate(pairs):
            copies.append(
                pltpu.make_async_copy(source.at[at], target.at[at], sems.at[part, index])
            )
    for copy in copies:
        copy.start()
    for piece in range(pieces):
        at = pl.ds(piece * LANES, LANES)
        if piece % half == 0:
            copies[3 * (piece // half)].wait()
            copies[3 * (piece // half) + 1].wait()
        product = key_ref[at, :].astype(F32) * value_ref[at, :].astype(F32)
        out_ref[:, piece, 0] = product.T.reshape(-1, share, LANES)
        if piece % half == 0:
            copies[3 * (piece // half) + 2].wait()
        out_ref[:, piece, 1] = filter_ref[at, :].T.reshape(-1, share, LANES)


def conv_kernel(
    group, share, data_ref, first_ref, turn_re_ref, turn_im_ref, fwd_ref, back_ref, last_ref, out_ref
):
    rows = turn_re_ref.shape[0]
    half = rows // 2
    turn_re = jnp.concatenate([turn_re_ref[...]] * 2, axis=1)
    turn_im = jnp.concatenate([turn_im_ref[...]] * 2, axis=1)

    def over_lanes(values, table_ref):
        high, low = split(values)
        return dot(jnp.concatenate([high, low, high], axis=1), table_ref[...])

    def half_sum(start, parity):
        signal = data_ref[pl.ds(2 * share * parity + start, half, stride=4 * share), :]
        kernel = data_ref[pl.ds(2 * share * parity + share + start, half, stride=4 * share), :]
        high, low = split(jnp.concatenate([signal, kernel], axis=1))
        table = first_ref[rows * parity : rows * (parity + 1)]
        return dot(table, jnp.concatenate([high, low, high], axis=0))

    def first_stage(start):
        parts = []
        for c in range(start, start + group):
            even, odd = half_sum(c, 0), half_sum(c, 1)
            total, difference = even + odd, even - odd
            re = jnp.concatenate([total[:half], difference[:half]], axis=0)
            im = jnp.concatenate([total[half:], difference[half:]], axis=0)
            out_re = re * turn_re - im * turn_im
            out_im = re * turn_im + im * turn_re
            parts.append(jnp.concatenate([out_re[:, :LANES], out_im[:, :LANES]], axis=1))
            parts.append(jnp.concatenate([out_re[:, LANES:], out_im[:, LANES:]], axis=1))
        return jnp.concatenate(parts, axis=0)

    def product_of_spectra(turned):
        spec = over_lanes(turned, fwd_ref)
        parts = []
        for c in range(group):
            signal = spec[2 * c * rows : (2 * c + 1) * rows]
            kernel = spec[(2 * c + 1) * rows : (2 * c + 2) * rows]
            s_re, s_im = signal[:, :LANES], signal[:, LANES:]
            k_re, k_im = kernel[:, :LANES], kernel[:, LANES:]
            parts.append(
                jnp.concatenate([s_re * k_re - s_im * k_im, s_re * k_im + s_im * k_re], axis=1)
            )
        return jnp.concatenate(parts, axis=0)

    def last_stage(spec, start):
        for c in range(0, group, 2):
            first = spec[c * rows : (c + 1) * rows]
            second = spec[(c + 1) * rows : (c + 2) * rows]
            re = jnp.concatenate([first[:, :LANES], second[:, :LANES]], axis=1)
            im = jnp.concatenate([first[:, LANES:], second[:, LANES:]], axis=1)
            turned = jnp.concatenate(
                [re * turn_re + im * turn_im, im * turn_re - re * turn_im], axis=0
            )
            high, low = split(turned)
            conv = dot(last_ref[...], high)
            conv = conv[:rows] + dot(last_ref[:rows], low) + conv[rows:]
            out_ref[pl.ds(start + c, rows, stride=share), :] = conv[:, :LANES]
            out_ref[pl.ds(start + c + 1, rows, stride=share), :] = conv[:, LANES:]

    groups = share // group
    turned, spectra, back = {}, {}, {}
    for step in range(groups + 3):
        if step < groups:
            turned[step] = first_stage(step * group)
        if 0 <= step - 1 < groups:
            spectra[step - 1] = product_of_spectra(turned.pop(step - 1))
        if 0 <= step - 2 < groups:
            back[step - 2] = over_lanes(spectra.pop(step - 2), back_ref)
        if 0 <= step - 3 < groups:
            last_stage(back.pop(step - 3), (step - 3) * group)


def gate_kernel(conv_ref, query_ref, key_ref, value_ref, skip_ref, gated_ref, square_ref):
    per_tile = LANES // conv_ref.shape[2]
    for piece in range(conv_ref.shape[1]):
        down = slice(piece * LANES, (piece + 1) * LANES)
        folded = None
        for tile in range(gated_ref.shape[1] // LANES):
            at = slice(tile * LANES, (tile + 1) * LANES)
            owners = slice(tile * per_tile, (tile + 1) * per_tile)
            conv = conv_ref[owners, piece].reshape(LANES, LANES).T
            product = key_ref[down, at].astype(F32) * value_ref[down, at].astype(F32)
            gated = query_ref[down, at].astype(F32) * (conv + skip_ref[:, at] * product)
            gated_ref[down, at] = gated
            square = gated * gated
            folded = square if folded is None else folded + square
        total = jnp.sum(folded.T, axis=0, keepdims=True)
        square_ref[:, down] = jnp.broadcast_to(total, (square_ref.shape[0], LANES))


def norm_kernel(gated_ref, square_ref, gain_ref, out_hbm, out_ref, sems):
    total = jnp.sum(square_ref[...], axis=0, keepdims=True)
    inverse = lax.rsqrt(total / CH + 1e-05)
    half = out_ref.shape[0] // 2
    sends = []
    for top in range(0, out_ref.shape[0], LANES):
        down = slice(top, top + LANES)
        spread = jnp.broadcast_to(inverse[:, down], (LANES, LANES)).T
        for start in range(0, out_ref.shape[1], LANES):
            at = slice(start, start + LANES)
            out_ref[down, at] = (gated_ref[down, at] * spread * gain_ref[:, at]).astype(BF16)
        if (top + LANES) % half == 0:
            part = pl.ds(top + LANES - half, half)
            sends.append(
                pltpu.make_async_copy(out_ref.at[part], out_hbm.at[part], sems.at[len(sends)])
            )
            sends[-1].start()
    for copy in sends:
        copy.wait()


def on_device(query_gate, key_branch, value_branch, conv_filter, skip_weight, norm_gain):
    blocks = lax.axis_size("ctx")
    peers = lax.axis_size("chan")
    tokens, channels = key_branch.shape
    share = channels // blocks
    pieces = tokens // LANES
    rows = blocks * pieces
    params = pltpu.CompilerParams(vmem_limit_bytes=VMEM_BYTES)
    strip = pl.BlockSpec((LANES, channels), lambda a: (a, 0))
    row = pl.BlockSpec((1, channels), lambda a: (0, 0))
    whole = (tokens, channels)
    packed_shape = (blocks, pieces, 2, share, LANES)
    inputs = [
        pltpu.with_memory_space_constraint(array, pltpu.HBM)
        for array in (key_branch, value_branch, conv_filter)
    ]
    packed = pl.pallas_call(
        pack_kernel,
        in_specs=[pl.BlockSpec(memory_space=pltpu.HBM)] * 3,
        out_specs=pl.BlockSpec(memory_space=pltpu.VMEM),
        out_shape=jax.ShapeDtypeStruct(packed_shape, F32),
        scratch_shapes=[
            pltpu.VMEM(whole, BF16),
            pltpu.VMEM(whole, BF16),
            pltpu.VMEM(whole, F32),
            pltpu.SemaphoreType.DMA((2, 3)),
        ],
        compiler_params=params,
        name="pack",
    )(*inputs)
    packed = packed.reshape(blocks, pieces * 2 * share, LANES)
    gathered = lax.all_to_all(packed, "ctx", split_axis=0, concat_axis=0, tiled=True)
    gathered = gathered.reshape(rows * 2 * share, LANES)
    tables = transform_tables(rows, LANES)
    conv = pl.pallas_call(
        functools.partial(conv_kernel, 2, share),
        out_shape=jax.ShapeDtypeStruct((rows * share, LANES), F32),
        compiler_params=params,
        name="conv",
    )(gathered, *tables)
    conv = conv.reshape(blocks, pieces * share, LANES)
    conv = lax.all_to_all(conv, "ctx", split_axis=0, concat_axis=0, tiled=True)
    conv = conv.reshape(blocks, pieces, share, LANES)
    gated, square = pl.pallas_call(
        gate_kernel,
        out_shape=[
            jax.ShapeDtypeStruct((tokens, channels), F32),
            jax.ShapeDtypeStruct((peers, tokens), F32),
        ],
        compiler_params=params,
        name="gate",
    )(conv, query_gate, key_branch, value_branch, skip_weight[None])
    square = lax.all_to_all(square, "chan", split_axis=0, concat_axis=0, tiled=True)
    return pl.pallas_call(
        norm_kernel,
        in_specs=[pl.BlockSpec(memory_space=pltpu.VMEM)] * 3,
        out_specs=pl.BlockSpec(memory_space=pltpu.HBM),
        out_shape=jax.ShapeDtypeStruct(whole, BF16),
        scratch_shapes=[pltpu.VMEM(whole, BF16), pltpu.SemaphoreType.DMA((2,))],
        compiler_params=params,
        name="norm",
    )(gated, square, norm_gain[None])


def solution(mesh):
    wide = P("ctx", "chan")
    return jax.shard_map(
        on_device,
        mesh=mesh,
        in_specs=(wide, wide, wide, wide, P("chan"), P("chan")),
        out_specs=wide,
        check_vma=False,
    )
```
